512 devices in a mesh: tm: 4 (over x), space: 128 (over z, y, core).
Axes of the slice: x: 4, y: 8, z: 8, core: 2. Of those that a mesh axis runs over, the one named last changes fastest.
Arguments:
- signal: bfloat16 [256, 256, 512], P('space', None, 'tm'), may hold values from -6 to 6
- source_boxes: int32 [256, 12], replicated, may hold values from 0 to 255
- near_boxes: int32 [256, 8], replicated, may hold values from 0 to 255, as said below
- trans_kernel: float32 [12, 256, 128], P(None, 'space'), may hold values from -0.15625 to 0.15625
- near_kernel: float32 [8, 128], replicated, may hold values from -0.1875 to 0.1875
Outputs:
- field: bfloat16 [256, 256, 512], P('space', None, 'tm')
The draws below stay inside these ranges and needn't reach their ends.
Inputs may be any that keep to these rules, and one draw needn't show every extreme that they name: Each near_boxes[b, j] lies within 2 of b.
All inputs are finite; a program needn't handle non-finite values.
Results may differ from the reference program's by a relative error of at most 0.008.
Values may be sent and summed in bfloat16 or wider, within the bound.
No kernel may reach another device: no remote copies, remote signals or barrier semaphores. Data moves between devices by JAX's collectives and lax.ppermute only.
A program may use at most 64 MiB of HBM per device.

```python
import jax
import jax.numpy as jnp
from jax import lax

R = 256
OFFSETS = 12
NEAR = 8
REACH = 2
TB = 128
BOXES = 256
SAMPLES = 512
N_TM = 4


def draw_near_boxes(key, part):
    boxes = jnp.arange(BOXES, dtype=jnp.int32)[:, None]
    moves = jax.random.randint(jax.random.fold_in(key, 17), (BOXES, NEAR), -REACH, REACH + 1, dtype=jnp.int32)
    return jnp.clip(boxes + moves, 0, BOXES - 1).astype(jnp.int32)


def plant(entries, rng, smallest, largest):
    longest = entries.shape.index(max(entries.shape))
    spots = []
    for shift in (0, 1):
        where = [jax.random.randint(jax.random.fold_in(rng, axis), (), 0, length) for axis, length in enumerate(entries.shape)]
        where[longest] = (where[longest] + shift) % entries.shape[longest]
        spots.append(tuple(where))
    return entries.at[spots[0]].set(smallest).at[spots[1]].set(largest)


def level_of(rng, shape, split, low, high):
    gain, own = 1.0, jax.random.fold_in(rng, 6)
    for position, blocks in split:
        draws = jnp.exp(jax.random.uniform(jax.random.fold_in(own, position), (blocks,), jnp.float32, low / len(split), high / len(split)))
        gain = gain * jnp.repeat(draws, shape[position] // blocks).reshape([-1 if axis == position else 1 for axis in range(len(shape))])
    return gain


def normal_values(stream_key, shape, spread, most, cuts=(), kind=jnp.bfloat16):
    loudness = level_of(stream_key, shape, cuts, -0.22, 0.18) if cuts else 1.0
    entries = jax.random.normal(stream_key, shape, jnp.float32) * spread * loudness
    return jnp.minimum(jnp.maximum(entries, -most), most).astype(kind)


def setup_inputs(seed: int = 0) -> dict:
    arg_keys = jax.random.split(jax.random.key(seed), 6)
    return {
        "signal": normal_values(arg_keys[0], (BOXES, R, SAMPLES), 1.0, 6.0, ((0, 128), (2, 4))),
        "source_boxes": plant(jax.random.randint(arg_keys[1], (BOXES, OFFSETS), 0, BOXES), jax.random.fold_in(arg_keys[1], 1), 0, BOXES - 1).astype(jnp.int32),
        "near_boxes": draw_near_boxes(jax.random.fold_in(arg_keys[5], 71), 0),
        "trans_kernel": normal_values(arg_keys[3], (OFFSETS, R, TB), (OFFSETS * TB) ** -0.5, 0.15625, ((1, 128),), jnp.float32),
        "near_kernel": normal_values(arg_keys[4], (NEAR, TB), (NEAR * TB) ** -0.5, 0.1875, (), jnp.float32),
    }


def block_matrix(kernel):
    width = kernel.shape[-1]
    rows = jnp.arange(2 * width, dtype=jnp.int32)[:, None]
    cols = jnp.arange(width, dtype=jnp.int32)[None, :]
    lagged = cols + width - rows
    valid = (lagged >= 0) & (lagged < width)
    clipped = jnp.clip(lagged, 0, width - 1)
    table = jnp.take(kernel, clipped, axis=-1)
    return jnp.where(valid, table, jnp.zeros_like(table)).astype(jnp.bfloat16)


def reference(signal, source_boxes, near_boxes, trans_kernel, near_kernel):
    blocks = signal.reshape(BOXES, R, N_TM, TB)
    earlier = jnp.concatenate([jnp.zeros_like(blocks[:, :, :1]), blocks[:, :, :-1]], axis=2)
    pair = jnp.concatenate([earlier, blocks], axis=-1)
    pair = jnp.transpose(pair, (1, 0, 2, 3))
    kernels = jnp.transpose(trans_kernel, (1, 0, 2))
    near_mats = block_matrix(near_kernel).astype(jnp.float32)

    def one_ray(inputs):
        rows, kernel = inputs
        trans_mats = block_matrix(kernel).astype(jnp.float32)
        rows32 = rows.astype(jnp.float32)
        far_rows = jnp.take(rows32, source_boxes, axis=0)
        far = jnp.einsum("bkms,kst->bmt", far_rows, trans_mats)
        near_rows = jnp.take(rows32, near_boxes, axis=0)
        near = jnp.einsum("bkms,kst->bmt", near_rows, near_mats)
        return far.astype(jnp.bfloat16), near.astype(jnp.bfloat16)

    far, near = lax.map(one_ray, (pair, kernels))
    field = (far.astype(jnp.float32) + near.astype(jnp.float32)).astype(jnp.bfloat16)
    field = jnp.transpose(field, (1, 0, 2, 3))
    return field.reshape(BOXES, R, SAMPLES)
```

```python
import functools

import jax
import jax.numpy as jnp
from jax import lax
from jax.experimental import pallas as pl
from jax.experimental.pallas import tpu as pltpu
from jax.sharding import PartitionSpec as P

VMEM = pl.BlockSpec(memory_space=pltpu.VMEM)


def circulant_halves(lags, dtype):
    width = lags.shape[-1]
    rows = jnp.broadcast_to(lags, (width, width))
    turned = pltpu.roll(rows, 0, 1, stride=1, stride_axis=0)
    s = lax.broadcasted_iota(jnp.int32, (width, width), 0)
    t = lax.broadcasted_iota(jnp.int32, (width, width), 1)
    before = jnp.where(t < s, turned, 0.0).astype(dtype)
    within = jnp.where(t >= s, turned, 0.0).astype(dtype)
    return before, within


def build_kernel(source_ref, near_ref, trans_ref, slot_ref, far_ref, near_mats_ref, pick_ref):
    offsets, rays, width = trans_ref.shape
    slots = slot_ref.shape[0]
    boxes = source_ref.shape[1]
    for r in range(rays):
        for k in range(offsets):
            before, within = circulant_halves(trans_ref[k, r : r + 1, :], jnp.bfloat16)
            far_ref[r, 0:width, k * width : (k + 1) * width] = before
            far_ref[r, width : 2 * width, k * width : (k + 1) * width] = within
    for j in range(slots):
        before, within = circulant_halves(slot_ref[j : j + 1, :], jnp.bfloat16)
        near_mats_ref[0:width, j * width : (j + 1) * width] = before
        near_mats_ref[width : 2 * width, j * width : (j + 1) * width] = within
    lane = lax.broadcasted_iota(jnp.int32, (boxes, boxes), 1)
    source = jnp.transpose(source_ref[...])
    near = jnp.transpose(near_ref[...])
    for k in range(offsets + slots):
        column = source[:, k : k + 1] if k < offsets else near[:, k - offsets : k - offsets + 1]
        hit = jnp.where(column == lane, 1.0, 0.0)
        pick_ref[:, k * boxes : (k + 1) * boxes] = hit.astype(jnp.bfloat16)


def field_kernel(cur_ref, prev_ref, far_ref, near_mats_ref, pick_ref, out_ref, wide, pair, mixed):
    rays, depth, far_cols = far_ref.shape
    width = depth // 2
    boxes = pick_ref.shape[0]
    offsets, slots = far_cols // width, near_mats_ref.shape[1] // width
    for half, ref in enumerate((prev_ref, cur_ref)):
        wide[...] = ref[...].astype(jnp.float32)
        for r in range(rays):
            rows = wide[pl.ds(r, boxes, stride=rays), :]
            pair[r, :, half * width : (half + 1) * width] = rows.astype(jnp.bfloat16)
    for r in range(rays):
        own = pair[r]
        lanes = slice(r * width, (r + 1) * width)
        for k in range(0, offsets + slots, 2):
            if k < offsets:
                mats = far_ref[r, :, k * width : (k + 2) * width]
            else:
                mats = near_mats_ref[:, (k - offsets) * width : (k - offsets + 2) * width]
            two = jnp.dot(own, mats, preferred_element_type=jnp.float32).astype(jnp.bfloat16)
            mixed[k * boxes : (k + 1) * boxes, lanes] = two[:, :width]
            mixed[(k + 1) * boxes : (k + 2) * boxes, lanes] = two[:, width:]
    cut = offsets * boxes
    far = jnp.dot(pick_ref[:, :cut], mixed[:cut, :], preferred_element_type=jnp.float32)
    near = jnp.dot(pick_ref[:, cut:], mixed[cut:, :], preferred_element_type=jnp.float32)
    far = far.astype(jnp.bfloat16).astype(jnp.float32)
    near = near.astype(jnp.bfloat16).astype(jnp.float32)
    both = far + near
    for r in range(rays):
        wide[pl.ds(r, boxes, stride=rays), :] = both[:, r * width : (r + 1) * width]
    out_ref[...] = wide[...].astype(jnp.bfloat16)


def body(signal, source_boxes, near_boxes, trans_kernel, near_kernel):
    box_dev, all_rays, width = signal.shape
    devs = lax.axis_size("space")
    rays = all_rays // devs
    boxes = box_dev * devs
    offsets, slots = trans_kernel.shape[0], near_kernel.shape[0]
    mid = box_dev * rays

    parted = signal.reshape(box_dev, devs, rays, width).transpose(1, 0, 2, 3).reshape(devs, mid, width)
    current = lax.all_to_all(parted, "space", split_axis=0, concat_axis=0, tiled=True)
    size = lax.axis_size("tm")
    earlier = lax.ppermute(current, "tm", [(i, i + 1) for i in range(size - 1)])

    far_mats, near_mats, picks = pl.pallas_call(
        build_kernel,
        out_shape=(
            jax.ShapeDtypeStruct((rays, 2 * width, offsets * width), jnp.bfloat16),
            jax.ShapeDtypeStruct((2 * width, slots * width), jnp.bfloat16),
            jax.ShapeDtypeStruct((boxes, (offsets + slots) * boxes), jnp.bfloat16),
        ),
        in_specs=[VMEM] * 4,
        out_specs=(VMEM,) * 3,
        compiler_params=pltpu.CompilerParams(vmem_limit_bytes=24 << 20),
        cost_estimate=pl.CostEstimate(flops=4_000_000, bytes_accessed=8_000_000, transcendentals=0),
        name="build",
    )(
        source_boxes.T,
        near_boxes.T,
        trans_kernel.astype(jnp.bfloat16).astype(jnp.float32),
        near_kernel.astype(jnp.bfloat16).astype(jnp.float32),
    )
    field = pl.pallas_call(
        field_kernel,
        out_shape=jax.ShapeDtypeStruct((devs * mid, width), jnp.bfloat16),
        in_specs=[VMEM] * 5,
        out_specs=VMEM,
        scratch_shapes=[
            pltpu.VMEM((devs * mid, width), jnp.float32),
            pltpu.VMEM((rays, boxes, 2 * width), jnp.bfloat16),
            pltpu.VMEM(((offsets + slots) * boxes, rays * width), jnp.bfloat16),
        ],
        compiler_params=pltpu.CompilerParams(vmem_limit_bytes=24 << 20),
        cost_estimate=pl.CostEstimate(flops=1_400_000_000, bytes_accessed=6_000_000, transcendentals=0),
        name="field",
    )(
        current.reshape(devs * mid, width),
        earlier.reshape(devs * mid, width),
        far_mats,
        near_mats,
        picks,
    )
    back = lax.all_to_all(field.reshape(devs, mid, width), "space", split_axis=0, concat_axis=0, tiled=True)
    back = back.reshape(devs, box_dev, rays, width).transpose(1, 0, 2, 3)
    return back.reshape(box_dev, all_rays, width)


def solution(mesh):
    in_specs = (P("space", None, "tm"), P(), P(), P(None, "space", None), P())
    out_specs = P("space", None, "tm")
    return jax.shard_map(body, mesh=mesh, in_specs=in_specs, out_specs=out_specs, check_vma=False)
```

```python
import functools

import jax
import jax.numpy as jnp
from jax import lax
from jax.experimental import pallas as pl
from jax.experimental.pallas import tpu as pltpu
from jax.sharding import PartitionSpec as P

VMEM = pl.BlockSpec(memory_space=pltpu.VMEM)
ANY = pl.BlockSpec(memory_space=pl.ANY)
Z, Y, CORES = 8, 8, 2
BATCH = Y // 2 * CORES


def ranks():
    return [((z + Z // 2) % Z * Y + (y + Y // 2) % Y) * CORES + c for z in range(Z) for y in range(Y) for c in range(CORES)]


def exchange(chunks):
    return lax.all_to_all(chunks, "space", split_axis=0, concat_axis=0, axis_index_groups=[ranks()], tiled=True)


def turned(box, z_half, y_half):
    half = Z // 2
    own = (box, pl.ds(z_half * half, half), y_half)
    there = (pl.ds((1 - z_half) * half, half), 1 - y_half, slice(None), box)
    return own, there


def parts_kernel(signal_ref, parts_ref, sems):
    copies = []
    for n in range(signal_ref.shape[0] * 4):
        own, there = turned(n // 4, n // 2 % 2, n % 2)
        copies.append(pltpu.make_async_copy(signal_ref.at[own], parts_ref.at[there], sems.at[n]))
    for copy in copies:
        copy.start()
    for copy in copies:
        copy.wait()


def whole_kernel(parts_ref, field_ref, sems):
    copies = []
    for n in range(field_ref.shape[0] * 4):
        own, there = turned(n // 4, n // 2 % 2, n % 2)
        copies.append(pltpu.make_async_copy(parts_ref.at[there], field_ref.at[own], sems.at[n]))
    for copy in copies:
        copy.start()
    for copy in copies:
        copy.wait()


def circulant_halves(lags, dtype):
    width = lags.shape[-1]
    rows = jnp.broadcast_to(lags.astype(dtype).astype(jnp.float32), (width, width))
    turned = pltpu.roll(rows, 0, 1, stride=1, stride_axis=0)
    s = lax.broadcasted_iota(jnp.int32, (width, width), 0)
    t = lax.broadcasted_iota(jnp.int32, (width, width), 1)
    before = jnp.where(t < s, turned, 0.0).astype(dtype)
    within = jnp.where(t >= s, turned, 0.0).astype(dtype)
    return before, within


def build_kernel(source_ref, near_ref, trans_ref, slot_ref, _, far_ref, near_mats_ref, pick_ref):
    offsets, rays, width = trans_ref.shape
    slots = slot_ref.shape[0]
    boxes = source_ref.shape[1]
    for r in range(rays):
        for k in range(offsets):
            before, within = circulant_halves(trans_ref[k, r : r + 1, :], jnp.bfloat16)
            far_ref[r, 0:width, k * width : (k + 1) * width] = before
            far_ref[r, width : 2 * width, k * width : (k + 1) * width] = within
    for j in range(slots):
        before, within = circulant_halves(slot_ref[j : j + 1, :], jnp.bfloat16)
        near_mats_ref[0:width, j * width : (j + 1) * width] = before
        near_mats_ref[width : 2 * width, j * width : (j + 1) * width] = within
    per_dev = boxes // (Z * Y * CORES)
    y_turn, z_turn = BATCH * per_dev, boxes // 2
    lane = lax.broadcasted_iota(jnp.int32, (boxes, boxes), 1) ^ (y_turn | z_turn)

    def by_rank(columns):
        runs = [(p ^ (y_turn | z_turn)) for p in range(0, boxes, y_turn)]
        return jnp.concatenate([columns[p : p + y_turn] for p in runs], axis=0)

    source = by_rank(jnp.transpose(source_ref[...]))
    near = by_rank(jnp.transpose(near_ref[...]))
    for k in range(offsets + slots):
        column = source[:, k : k + 1] if k < offsets else near[:, k - offsets : k - offsets + 1]
        hit = jnp.where(column == lane, 1.0, 0.0)
        pick_ref[:, k * boxes : (k + 1) * boxes] = hit.astype(jnp.bfloat16)


def field_kernel(cur_ref, prev_ref, far_ref, near_mats_ref, pick_ref, out_ref, wide, pair, mixed):
    rays, depth, far_cols = far_ref.shape
    width = depth // 2
    boxes = pick_ref.shape[0]
    offsets, slots = far_cols // width, near_mats_ref.shape[1] // width
    for half, ref in enumerate((prev_ref, cur_ref)):
        wide[...] = ref[...].astype(jnp.float32)
        for r in range(rays):
            rows = wide[pl.ds(r, boxes, stride=rays), :]
            pair[r, :, half * width : (half + 1) * width] = rows.astype(jnp.bfloat16)
    for r in range(rays):
        own = pair[r]
        lanes = slice(r * width, (r + 1) * width)
        for k in range(0, offsets + slots, 2):
            if k < offsets:
                mats = far_ref[r, :, k * width : (k + 2) * width]
            else:
                mats = near_mats_ref[:, (k - offsets) * width : (k - offsets + 2) * width]
            two = jnp.dot(own, mats, preferred_element_type=jnp.float32).astype(jnp.bfloat16)
            mixed[k * boxes : (k + 1) * boxes, lanes] = two[:, :width]
            mixed[(k + 1) * boxes : (k + 2) * boxes, lanes] = two[:, width:]
    cut = offsets * boxes
    far = jnp.dot(pick_ref[:, :cut], mixed[:cut, :], preferred_element_type=jnp.float32)
    near = jnp.dot(pick_ref[:, cut:], mixed[cut:, :], preferred_element_type=jnp.float32)
    far = far.astype(jnp.bfloat16).astype(jnp.float32)
    near = near.astype(jnp.bfloat16).astype(jnp.float32)
    both = far + near
    for r in range(rays):
        wide[pl.ds(r, boxes, stride=rays), :] = both[:, r * width : (r + 1) * width]
    out_ref[...] = wide[...].astype(jnp.bfloat16)


def body(signal, source_boxes, near_boxes, trans_kernel, near_kernel):
    box_dev, all_rays, width = signal.shape
    devs = lax.axis_size("space")
    rays = all_rays // devs
    boxes = box_dev * devs
    offsets, slots = trans_kernel.shape[0], near_kernel.shape[0]
    mid = box_dev * rays

    split = (box_dev, Z, 2, BATCH, rays, width)
    parted = pl.pallas_call(
        parts_kernel,
        out_shape=jax.ShapeDtypeStruct((Z, 2, BATCH, box_dev, rays, width), signal.dtype),
        in_specs=[ANY],
        out_specs=VMEM,
        scratch_shapes=[pltpu.SemaphoreType.DMA((4 * box_dev,))],
        compiler_params=pltpu.CompilerParams(vmem_limit_bytes=4 << 20),
        name="parts",
    )(signal.reshape(split))
    current = exchange(parted.reshape(devs, mid, width))
    size = lax.axis_size("tm")
    earlier = lax.ppermute(current, "tm", [(i, i + 1) for i in range(size - 1)])

    far_mats, near_mats, picks = pl.pallas_call(
        build_kernel,
        out_shape=(
            jax.ShapeDtypeStruct((rays, 2 * width, offsets * width), jnp.bfloat16),
            jax.ShapeDtypeStruct((2 * width, slots * width), jnp.bfloat16),
            jax.ShapeDtypeStruct((boxes, (offsets + slots) * boxes), jnp.bfloat16),
        ),
        in_specs=[VMEM] * 4 + [ANY],
        out_specs=(VMEM,) * 3,
        compiler_params=pltpu.CompilerParams(vmem_limit_bytes=24 << 20),
        cost_estimate=pl.CostEstimate(flops=4_000_000, bytes_accessed=8_000_000, transcendentals=0),
        name="build",
    )(
        source_boxes.T,
        near_boxes.T,
        trans_kernel,
        near_kernel,
        current,
    )
    field = pl.pallas_call(
        field_kernel,
        out_shape=jax.ShapeDtypeStruct((devs * mid, width), jnp.bfloat16),
        in_specs=[VMEM] * 5,
        out_specs=VMEM,
        scratch_shapes=[
            pltpu.VMEM((devs * mid, width), jnp.float32),
            pltpu.VMEM((rays, boxes, 2 * width), jnp.bfloat16),
            pltpu.VMEM(((offsets + slots) * boxes, rays * width), jnp.bfloat16),
        ],
        compiler_params=pltpu.CompilerParams(vmem_limit_bytes=24 << 20),
        cost_estimate=pl.CostEstimate(flops=1_400_000_000, bytes_accessed=6_000_000, transcendentals=0),
        name="field",
    )(
        current.reshape(devs * mid, width),
        earlier.reshape(devs * mid, width),
        far_mats,
        near_mats,
        picks,
    )
    back = exchange(field.reshape(devs, mid, width))
    whole = pl.pallas_call(
        whole_kernel,
        out_shape=jax.ShapeDtypeStruct(split, signal.dtype),
        in_specs=[VMEM],
        out_specs=ANY,
        scratch_shapes=[pltpu.SemaphoreType.DMA((4 * box_dev,))],
        compiler_params=pltpu.CompilerParams(vmem_limit_bytes=4 << 20),
        name="whole",
    )(back.reshape(Z, 2, BATCH, box_dev, rays, width))
    return whole.reshape(signal.shape)


def solution(mesh):
    in_specs = (P("space", None, "tm"), P(), P(), P(None, "space", None), P())
    out_specs = P("space", None, "tm")
    return jax.shard_map(body, mesh=mesh, in_specs=in_specs, out_specs=out_specs, check_vma=False)
```

```python
import functools

import jax
import jax.numpy as jnp
from jax import lax
from jax.experimental import pallas as pl
from jax.experimental.pallas import tpu as pltpu
from jax.sharding import PartitionSpec as P

VMEM = pl.BlockSpec(memory_space=pltpu.VMEM)
HBM = pl.BlockSpec(memory_space=pltpu.HBM)
Z, Y, CORES = 8, 8, 2
BATCH = Y // 2 * CORES


def in_hbm(array):
    return pltpu.with_memory_space_constraint(array, pltpu.HBM)


def ranks():
    return [((z + Z // 2) % Z * Y + (y + Y // 2) % Y) * CORES + c for z in range(Z) for y in range(Y) for c in range(CORES)]


def exchange(chunks):
    return lax.all_to_all(chunks, "space", split_axis=0, concat_axis=0, axis_index_groups=[ranks()], tiled=True)


def turned(box, z_half, y_half):
    half = Z // 2
    own = (box, pl.ds(z_half * half, half), y_half)
    there = (pl.ds((1 - z_half) * half, half), 1 - y_half, slice(None), box)
    return own, there


def parts_kernel(signal_ref, parts_ref, sems):
    copies = []
    for n in range(signal_ref.shape[0] * 4):
        own, there = turned(n // 4, n // 2 % 2, n % 2)
        copies.append(pltpu.make_async_copy(signal_ref.at[own], parts_ref.at[there], sems.at[n]))
    for copy in copies:
        copy.start()
    for copy in copies:
        copy.wait()


def whole_kernel(parts_ref, field_ref, sems):
    copies = []
    for n in range(field_ref.shape[0] * 4):
        own, there = turned(n // 4, n // 2 % 2, n % 2)
        copies.append(pltpu.make_async_copy(parts_ref.at[there], field_ref.at[own], sems.at[n]))
    for copy in copies:
        copy.start()
    for copy in copies:
        copy.wait()


def circulant_halves(lags):
    width = lags.shape[-1]
    lags = lags.astype(jnp.bfloat16).astype(jnp.float32)
    turned = pltpu.roll(jnp.broadcast_to(lags, (width, width)), 0, 1, stride=1, stride_axis=0)
    s = lax.broadcasted_iota(jnp.int32, (width, width), 0)
    t = lax.broadcasted_iota(jnp.int32, (width, width), 1)
    before = jnp.where(t < s, turned, 0.0).astype(jnp.bfloat16)
    within = jnp.where(t >= s, turned, 0.0).astype(jnp.bfloat16)
    return before, within


def rows_of_rays(block_ref, wide, rows):
    rays, boxes, _ = rows.shape
    wide[...] = block_ref[...].astype(jnp.float32)
    for r in range(rays):
        rows[r] = wide[pl.ds(r, boxes, stride=rays), :].astype(jnp.bfloat16)


def mix(rows, far_ref, slot_ref, mixed):
    rays, boxes, width = rows.shape
    offsets, slots = far_ref.shape[2] // width, slot_ref.shape[1] // width
    for r in range(rays):
        own = rows[r]
        lanes = slice(r * width, (r + 1) * width)
        for k in range(0, offsets + slots, 2):
            if k < offsets:
                mats = far_ref[r, :, k * width : (k + 2) * width]
            else:
                mats = slot_ref[:, (k - offsets) * width : (k - offsets + 2) * width]
            two = jnp.dot(own, mats, preferred_element_type=jnp.float32).astype(jnp.bfloat16)
            mixed[k * boxes : (k + 1) * boxes, lanes] = two[:, :width]
            mixed[(k + 1) * boxes : (k + 2) * boxes, lanes] = two[:, width:]


def pick(pick_ref, mixed, cut):
    far = jnp.dot(pick_ref[:, :cut], mixed[:cut, :], preferred_element_type=jnp.float32)
    near = jnp.dot(pick_ref[:, cut:], mixed[cut:, :], preferred_element_type=jnp.float32)
    return far, near


def current_kernel(
    source_hbm, near_hbm, trans_hbm, slot_hbm, cur_ref, far_before, slot_before, pick_ref, sums_ref,
    source_ref, near_ref, trans_ref, slot_ref, sems, far_within, slot_within, wide, rows, mixed,
):
    given, held = (source_hbm, near_hbm, trans_hbm, slot_hbm), (source_ref, near_ref, trans_ref, slot_ref)
    copies = [pltpu.make_async_copy(ref, here, sems.at[n]) for n, (ref, here) in enumerate(zip(given, held))]
    for copy in copies:
        copy.start()
    rows_of_rays(cur_ref, wide, rows)
    for copy in copies:
        copy.wait()
    offsets, rays, width = trans_ref.shape
    slots = slot_ref.shape[0]
    boxes = source_ref.shape[1]
    for k in range(offsets):
        for r in range(rays):
            before, within = circulant_halves(trans_ref[k, r : r + 1, :])
            far_before[r, :, k * width : (k + 1) * width] = before
            far_within[r, :, k * width : (k + 1) * width] = within
    for j in range(slots):
        before, within = circulant_halves(slot_ref[j : j + 1, :])
        slot_before[:, j * width : (j + 1) * width] = before
        slot_within[:, j * width : (j + 1) * width] = within
    per_dev = boxes // (Z * Y * CORES)
    y_turn, z_turn = BATCH * per_dev, boxes // 2
    lane = lax.broadcasted_iota(jnp.int32, (boxes, boxes), 1) ^ (y_turn | z_turn)

    def by_rank(columns):
        runs = [(p ^ (y_turn | z_turn)) for p in range(0, boxes, y_turn)]
        return jnp.concatenate([columns[p : p + y_turn] for p in runs], axis=0)

    source = by_rank(jnp.transpose(source_ref[...]))
    near = by_rank(jnp.transpose(near_ref[...]))
    for k in range(offsets + slots):
        column = source[:, k : k + 1] if k < offsets else near[:, k - offsets : k - offsets + 1]
        hit = jnp.where(column == lane, 1.0, 0.0)
        pick_ref[:, k * boxes : (k + 1) * boxes] = hit.astype(jnp.bfloat16)
    mix(rows, far_within, slot_within, mixed)
    sums_ref[0], sums_ref[1] = pick(pick_ref, mixed, offsets * boxes)


def earlier_kernel(prev_ref, far_before, slot_before, pick_ref, sums_ref, out_ref, wide, rows, mixed):
    rays, width, far_cols = far_before.shape
    boxes = pick_ref.shape[0]
    rows_of_rays(prev_ref, wide, rows)
    mix(rows, far_before, slot_before, mixed)
    far, near = pick(pick_ref, mixed, far_cols // width * boxes)
    far = (sums_ref[0] + far).astype(jnp.bfloat16).astype(jnp.float32)
    near = (sums_ref[1] + near).astype(jnp.bfloat16).astype(jnp.float32)
    both = far + near
    for r in range(rays):
        wide[pl.ds(r, boxes, stride=rays), :] = both[:, r * width : (r + 1) * width]
    out_ref[...] = wide[...].astype(jnp.bfloat16)


def body(signal, source_boxes, near_boxes, trans_kernel, near_kernel):
    box_dev, all_rays, width = signal.shape
    devs = lax.axis_size("space")
    rays = all_rays // devs
    boxes = box_dev * devs
    offsets, slots = trans_kernel.shape[0], near_kernel.shape[0]
    mid = box_dev * rays

    split = (box_dev, Z, 2, BATCH, rays, width)
    parted = pl.pallas_call(
        parts_kernel,
        out_shape=jax.ShapeDtypeStruct((Z, 2, BATCH, box_dev, rays, width), signal.dtype),
        in_specs=[HBM],
        out_specs=VMEM,
        scratch_shapes=[pltpu.SemaphoreType.DMA((4 * box_dev,))],
        compiler_params=pltpu.CompilerParams(vmem_limit_bytes=4 << 20),
        name="parts",
    )(in_hbm(signal.reshape(split)))
    current = exchange(parted.reshape(devs, mid, width))
    size = lax.axis_size("tm")
    earlier = lax.ppermute(current, "tm", [(i, i + 1) for i in range(size - 1)])

    far_before = jax.ShapeDtypeStruct((rays, width, offsets * width), jnp.bfloat16)
    slot_before = jax.ShapeDtypeStruct((width, slots * width), jnp.bfloat16)
    work = [
        pltpu.VMEM((devs * mid, width), jnp.float32),
        pltpu.VMEM((rays, boxes, width), jnp.bfloat16),
        pltpu.VMEM(((offsets + slots) * boxes, rays * width), jnp.bfloat16),
    ]
    begun = pl.pallas_call(
        current_kernel,
        out_shape=(
            far_before,
            slot_before,
            jax.ShapeDtypeStruct((boxes, (offsets + slots) * boxes), jnp.bfloat16),
            jax.ShapeDtypeStruct((2, boxes, rays * width), jnp.float32),
        ),
        in_specs=[HBM] * 4 + [VMEM],
        out_specs=(VMEM,) * 4,
        scratch_shapes=[
            pltpu.VMEM((offsets, boxes), jnp.int32),
            pltpu.VMEM((slots, boxes), jnp.int32),
            pltpu.VMEM(trans_kernel.shape, jnp.float32),
            pltpu.VMEM(near_kernel.shape, jnp.float32),
            pltpu.SemaphoreType.DMA((4,)),
            pltpu.VMEM(far_before.shape, jnp.bfloat16),
            pltpu.VMEM(slot_before.shape, jnp.bfloat16),
            *work,
        ],
        compiler_params=pltpu.CompilerParams(vmem_limit_bytes=24 << 20),
        cost_estimate=pl.CostEstimate(flops=1_000_000_000, bytes_accessed=6_000_000, transcendentals=0),
        name="current",
    )(
        in_hbm(source_boxes.T),
        in_hbm(near_boxes.T),
        in_hbm(trans_kernel),
        in_hbm(near_kernel),
        current.reshape(devs * mid, width),
    )
    field = pl.pallas_call(
        earlier_kernel,
        out_shape=jax.ShapeDtypeStruct((devs * mid, width), jnp.bfloat16),
        in_specs=[VMEM] * 5,
        out_specs=VMEM,
        scratch_shapes=work,
        compiler_params=pltpu.CompilerParams(vmem_limit_bytes=24 << 20),
        cost_estimate=pl.CostEstimate(flops=1_000_000_000, bytes_accessed=6_000_000, transcendentals=0),
        name="earlier",
    )(earlier.reshape(devs * mid, width), *begun)
    back = exchange(field.reshape(devs, mid, width))
    whole = pl.pallas_call(
        whole_kernel,
        out_shape=jax.ShapeDtypeStruct(split, signal.dtype),
        in_specs=[VMEM],
        out_specs=pl.BlockSpec(memory_space=pl.ANY),
        scratch_shapes=[pltpu.SemaphoreType.DMA((4 * box_dev,))],
        compiler_params=pltpu.CompilerParams(vmem_limit_bytes=4 << 20),
        name="whole",
    )(back.reshape(Z, 2, BATCH, box_dev, rays, width))
    return whole.reshape(signal.shape)


def solution(mesh):
    in_specs = (P("space", None, "tm"), P(), P(), P(None, "space", None), P())
    out_specs = P("space", None, "tm")
    return jax.shard_map(body, mesh=mesh, in_specs=in_specs, out_specs=out_specs, check_vma=False)
```

```python
import functools

import jax
import jax.numpy as jnp
from jax import lax
from jax.experimental import pallas as pl
from jax.experimental.pallas import tpu as pltpu
from jax.sharding import PartitionSpec as P

VMEM = pl.BlockSpec(memory_space=pltpu.VMEM)
HBM = pl.BlockSpec(memory_space=pltpu.HBM)
Z, Y, CORES = 8, 8, 2
TURNS = (4, 0, 6, 2, 5, 1, 7, 3)
CHIPS = [z * Y + y for y in TURNS for z in TURNS]
RANKS = [chip * CORES + c for chip in CHIPS for c in range(CORES)]


def in_hbm(array):
    return pltpu.with_memory_space_constraint(array, pltpu.HBM)


def exchange(chunks):
    return lax.all_to_all(chunks, "space", split_axis=0, concat_axis=0, axis_index_groups=[RANKS], tiled=True)


def parts_kernel(signal_hbm, parts_ref, signal_ref, sem):
    copy = pltpu.make_async_copy(signal_hbm, signal_ref, sem)
    copy.start()
    copy.wait()
    for rank, dev in enumerate(RANKS):
        for box in range(signal_ref.shape[0]):
            parts_ref[rank, box] = signal_ref[box, dev]


def whole_kernel(parts_ref, field_hbm, field_ref, sem):
    for rank, dev in enumerate(RANKS):
        for box in range(field_ref.shape[0]):
            field_ref[box, dev] = parts_ref[rank, box]
    copy = pltpu.make_async_copy(field_ref, field_hbm, sem)
    copy.start()
    copy.wait()


def circulant_halves(lags):
    width = lags.shape[-1]
    lags = lags.astype(jnp.bfloat16).astype(jnp.float32)
    turned = pltpu.roll(jnp.broadcast_to(lags, (width, width)), 0, 1, stride=1, stride_axis=0)
    s = lax.broadcasted_iota(jnp.int32, (width, width), 0)
    t = lax.broadcasted_iota(jnp.int32, (width, width), 1)
    before = jnp.where(t < s, turned, 0.0).astype(jnp.bfloat16)
    within = jnp.where(t >= s, turned, 0.0).astype(jnp.bfloat16)
    return before, within


def rows_of_rays(block_ref, wide, rows):
    rays, boxes, _ = rows.shape
    run = wide.shape[0] // len(CHIPS)
    for n in range(0, len(CHIPS), 2):
        two = block_ref[n * run : (n + 2) * run, :].astype(jnp.float32)
        for chip, one in ((CHIPS[n], two[:run]), (CHIPS[n + 1], two[run:])):
            wide[chip * run : (chip + 1) * run, :] = one
    for r in range(rays):
        rows[r] = wide[pl.ds(r, boxes, stride=rays), :].astype(jnp.bfloat16)


def mix(rows, far_ref, slot_ref, mixed):
    rays, boxes, width = rows.shape
    offsets, slots = far_ref.shape[2] // width, slot_ref.shape[1] // width
    for r in range(rays):
        own = rows[r]
        lanes = slice(r * width, (r + 1) * width)
        for k in range(0, offsets + slots, 2):
            if k < offsets:
                mats = far_ref[r, :, k * width : (k + 2) * width]
            else:
                mats = slot_ref[:, (k - offsets) * width : (k - offsets + 2) * width]
            two = jnp.dot(own, mats, preferred_element_type=jnp.float32).astype(jnp.bfloat16)
            mixed[k * boxes : (k + 1) * boxes, lanes] = two[:, :width]
            mixed[(k + 1) * boxes : (k + 2) * boxes, lanes] = two[:, width:]


def pick(pick_ref, mixed, cut):
    far = jnp.dot(pick_ref[:, :cut], mixed[:cut, :], preferred_element_type=jnp.float32)
    near = jnp.dot(pick_ref[:, cut:], mixed[cut:, :], preferred_element_type=jnp.float32)
    return far, near


def current_kernel(
    source_hbm, near_hbm, trans_hbm, slot_hbm, cur_ref, far_before, slot_before, pick_ref, sums_ref,
    source_ref, near_ref, trans_ref, slot_ref, sems, far_within, slot_within, wide, rows, mixed,
):
    given, held = (source_hbm, near_hbm, trans_hbm, slot_hbm), (source_ref, near_ref, trans_ref, slot_ref)
    copies = [pltpu.make_async_copy(ref, here, sems.at[n]) for n, (ref, here) in enumerate(zip(given, held))]
    for copy in copies:
        copy.start()
    rows_of_rays(cur_ref, wide, rows)
    for copy in copies:
        copy.wait()
    offsets, rays, width = trans_ref.shape
    slots = slot_ref.shape[0]
    boxes = source_ref.shape[1]
    for k in range(offsets):
        for r in range(rays):
            before, within = circulant_halves(trans_ref[k, r : r + 1, :])
            far_before[r, :, k * width : (k + 1) * width] = before
            far_within[r, :, k * width : (k + 1) * width] = within
    for j in range(slots):
        before, within = circulant_halves(slot_ref[j : j + 1, :])
        slot_before[:, j * width : (j + 1) * width] = before
        slot_within[:, j * width : (j + 1) * width] = within
    lane = lax.broadcasted_iota(jnp.int32, (boxes, boxes), 1)
    source = jnp.transpose(source_ref[...])
    near = jnp.transpose(near_ref[...])
    for k in range(offsets + slots):
        column = source[:, k : k + 1] if k < offsets else near[:, k - offsets : k - offsets + 1]
        hit = jnp.where(column == lane, 1.0, 0.0)
        pick_ref[:, k * boxes : (k + 1) * boxes] = hit.astype(jnp.bfloat16)
    mix(rows, far_within, slot_within, mixed)
    sums_ref[0], sums_ref[1] = pick(pick_ref, mixed, offsets * boxes)


def earlier_kernel(prev_ref, far_before, slot_before, pick_ref, sums_ref, out_ref, wide, rows, mixed):
    rays, width, far_cols = far_before.shape
    boxes = pick_ref.shape[0]
    rows_of_rays(prev_ref, wide, rows)
    mix(rows, far_before, slot_before, mixed)
    far, near = pick(pick_ref, mixed, far_cols // width * boxes)
    far = (sums_ref[0] + far).astype(jnp.bfloat16).astype(jnp.float32)
    near = (sums_ref[1] + near).astype(jnp.bfloat16).astype(jnp.float32)
    both = far + near
    for r in range(rays):
        wide[pl.ds(r, boxes, stride=rays), :] = both[:, r * width : (r + 1) * width]
    run = wide.shape[0] // len(CHIPS)
    for n in range(0, len(CHIPS), 2):
        two = [wide[chip * run : (chip + 1) * run, :] for chip in CHIPS[n : n + 2]]
        out_ref[n * run : (n + 2) * run, :] = jnp.concatenate(two, axis=0).astype(jnp.bfloat16)


def body(signal, source_boxes, near_boxes, trans_kernel, near_kernel):
    box_dev, all_rays, width = signal.shape
    devs = lax.axis_size("space")
    rays = all_rays // devs
    boxes = box_dev * devs
    offsets, slots = trans_kernel.shape[0], near_kernel.shape[0]
    mid = box_dev * rays

    split = (box_dev, devs, rays, width)
    parted = pl.pallas_call(
        parts_kernel,
        out_shape=jax.ShapeDtypeStruct((devs, box_dev, rays, width), signal.dtype),
        in_specs=[HBM],
        out_specs=VMEM,
        scratch_shapes=[pltpu.VMEM(split, signal.dtype), pltpu.SemaphoreType.DMA],
        compiler_params=pltpu.CompilerParams(vmem_limit_bytes=4 << 20),
        name="parts",
    )(in_hbm(signal.reshape(split)))
    current = exchange(parted.reshape(devs, mid, width))
    size = lax.axis_size("tm")
    earlier = lax.ppermute(current, "tm", [(i, i + 1) for i in range(size - 1)])

    far_before = jax.ShapeDtypeStruct((rays, width, offsets * width), jnp.bfloat16)
    slot_before = jax.ShapeDtypeStruct((width, slots * width), jnp.bfloat16)
    work = [
        pltpu.VMEM((devs * mid, width), jnp.float32),
        pltpu.VMEM((rays, boxes, width), jnp.bfloat16),
        pltpu.VMEM(((offsets + slots) * boxes, rays * width), jnp.bfloat16),
    ]
    begun = pl.pallas_call(
        current_kernel,
        out_shape=(
            far_before,
            slot_before,
            jax.ShapeDtypeStruct((boxes, (offsets + slots) * boxes), jnp.bfloat16),
            jax.ShapeDtypeStruct((2, boxes, rays * width), jnp.float32),
        ),
        in_specs=[HBM] * 4 + [VMEM],
        out_specs=(VMEM,) * 4,
        scratch_shapes=[
            pltpu.VMEM((offsets, boxes), jnp.int32),
            pltpu.VMEM((slots, boxes), jnp.int32),
            pltpu.VMEM(trans_kernel.shape, jnp.float32),
            pltpu.VMEM(near_kernel.shape, jnp.float32),
            pltpu.SemaphoreType.DMA((4,)),
            pltpu.VMEM(far_before.shape, jnp.bfloat16),
            pltpu.VMEM(slot_before.shape, jnp.bfloat16),
            *work,
        ],
        compiler_params=pltpu.CompilerParams(vmem_limit_bytes=24 << 20),
        cost_estimate=pl.CostEstimate(flops=1_000_000_000, bytes_accessed=6_000_000, transcendentals=0),
        name="current",
    )(
        in_hbm(source_boxes.T),
        in_hbm(near_boxes.T),
        in_hbm(trans_kernel),
        in_hbm(near_kernel),
        current.reshape(devs * mid, width),
    )
    field = pl.pallas_call(
        earlier_kernel,
        out_shape=jax.ShapeDtypeStruct((devs * mid, width), jnp.bfloat16),
        in_specs=[VMEM] * 5,
        out_specs=VMEM,
        scratch_shapes=work,
        compiler_params=pltpu.CompilerParams(vmem_limit_bytes=24 << 20),
        cost_estimate=pl.CostEstimate(flops=1_000_000_000, bytes_accessed=6_000_000, transcendentals=0),
        name="earlier",
    )(earlier.reshape(devs * mid, width), *begun)
    back = exchange(field.reshape(devs, mid, width))
    whole = pl.pallas_call(
        whole_kernel,
        out_shape=jax.ShapeDtypeStruct(split, signal.dtype),
        in_specs=[VMEM],
        out_specs=pl.BlockSpec(memory_space=pl.ANY),
        scratch_shapes=[pltpu.VMEM(split, signal.dtype), pltpu.SemaphoreType.DMA],
        compiler_params=pltpu.CompilerParams(vmem_limit_bytes=4 << 20),
        name="whole",
    )(back.reshape(devs, box_dev, rays, width))
    return whole.reshape(signal.shape)


def solution(mesh):
    in_specs = (P("space", None, "tm"), P(), P(), P(None, "space", None), P())
    out_specs = P("space", None, "tm")
    return jax.shard_map(body, mesh=mesh, in_specs=in_specs, out_specs=out_specs, check_vma=False)
```

```python
import functools

import jax
import jax.numpy as jnp
from jax import lax
from jax.experimental import pallas as pl
from jax.experimental.pallas import tpu as pltpu
from jax.sharding import PartitionSpec as P

VMEM = pl.BlockSpec(memory_space=pltpu.VMEM)
HBM = pl.BlockSpec(memory_space=pltpu.HBM)
Z, Y, CORES = 8, 8, 2
TURNS = (4, 0, 6, 2, 5, 1, 7, 3)
CHIPS = [z * Y + y for y in TURNS for z in TURNS]
RANKS = [chip * CORES + c for chip in CHIPS for c in range(CORES)]


def in_hbm(array):
    return pltpu.with_memory_space_constraint(array, pltpu.HBM)


def exchange(chunks):
    return lax.all_to_all(chunks, "space", split_axis=0, concat_axis=0, axis_index_groups=[RANKS], tiled=True)


def parts_kernel(signal_hbm, parts_ref, signal_ref, sem):
    copy = pltpu.make_async_copy(signal_hbm, signal_ref, sem)
    copy.start()
    copy.wait()
    for rank, dev in enumerate(RANKS):
        for box in range(signal_ref.shape[0]):
            parts_ref[rank, box] = signal_ref[box, dev]


def whole_kernel(parts_ref, field_hbm, field_ref, sem):
    for rank, dev in enumerate(RANKS):
        for box in range(field_ref.shape[0]):
            field_ref[box, dev] = parts_ref[rank, box]
    copy = pltpu.make_async_copy(field_ref, field_hbm, sem)
    copy.start()
    copy.wait()


def circulant_halves(lags):
    width = lags.shape[-1]
    lags = lags.astype(jnp.bfloat16).astype(jnp.float32)
    turned = pltpu.roll(jnp.broadcast_to(lags, (width, width)), 0, 1, stride=1, stride_axis=0)
    s = lax.broadcasted_iota(jnp.int32, (width, width), 0)
    t = lax.broadcasted_iota(jnp.int32, (width, width), 1)
    before = jnp.where(t < s, turned, 0.0).astype(jnp.bfloat16)
    within = jnp.where(t >= s, turned, 0.0).astype(jnp.bfloat16)
    return before, within


def rows_of_rays(block_ref, wide, rows):
    rays, boxes, _ = rows.shape
    run = wide.shape[0] // len(CHIPS)
    for n in range(0, len(CHIPS), 2):
        two = block_ref[n * run : (n + 2) * run, :].astype(jnp.float32)
        for chip, one in ((CHIPS[n], two[:run]), (CHIPS[n + 1], two[run:])):
            wide[chip * run : (chip + 1) * run, :] = one
    for r in range(rays):
        rows[r] = wide[pl.ds(r, boxes, stride=rays), :].astype(jnp.bfloat16)


def sums_of(rows, far_ref, slot_ref, pick_ref, taken):
    rays, boxes, width = rows.shape
    offsets, slots = far_ref.shape[1] // width, slot_ref.shape[0] // width
    beside = jnp.concatenate([rows[r] for r in range(rays)], axis=1)
    for k in range(offsets + slots):
        got = jnp.dot(pick_ref[k * boxes : (k + 1) * boxes, :], beside, preferred_element_type=jnp.float32)
        got = got.astype(jnp.bfloat16)
        for r in range(rays):
            taken[r, :, k * width : (k + 1) * width] = got[:, r * width : (r + 1) * width]
    cut = offsets * width
    return [
        (
            jnp.dot(taken[r, :, :cut], far_ref[r], preferred_element_type=jnp.float32),
            jnp.dot(taken[r, :, cut:], slot_ref[...], preferred_element_type=jnp.float32),
        )
        for r in range(rays)
    ]


def current_kernel(
    source_hbm, near_hbm, trans_hbm, slot_hbm, cur_ref, far_before, slot_before, pick_ref, sums_ref,
    source_ref, near_ref, trans_ref, slot_ref, sems, far_within, slot_within, wide, rows, taken,
):
    given, held = (source_hbm, near_hbm, trans_hbm, slot_hbm), (source_ref, near_ref, trans_ref, slot_ref)
    copies = [pltpu.make_async_copy(ref, here, sems.at[n]) for n, (ref, here) in enumerate(zip(given, held))]
    for copy in copies:
        copy.start()
    rows_of_rays(cur_ref, wide, rows)
    for copy in copies:
        copy.wait()
    offsets, rays, width = trans_ref.shape
    slots = slot_ref.shape[0]
    boxes = source_ref.shape[1]
    for k in range(offsets):
        for r in range(rays):
            before, within = circulant_halves(trans_ref[k, r : r + 1, :])
            far_before[r, k * width : (k + 1) * width, :] = before
            far_within[r, k * width : (k + 1) * width, :] = within
    for j in range(slots):
        before, within = circulant_halves(slot_ref[j : j + 1, :])
        slot_before[j * width : (j + 1) * width, :] = before
        slot_within[j * width : (j + 1) * width, :] = within
    lane = lax.broadcasted_iota(jnp.int32, (boxes, boxes), 1)
    source = jnp.transpose(source_ref[...])
    near = jnp.transpose(near_ref[...])
    for k in range(offsets + slots):
        column = source[:, k : k + 1] if k < offsets else near[:, k - offsets : k - offsets + 1]
        hit = jnp.where(column == lane, 1.0, 0.0)
        pick_ref[k * boxes : (k + 1) * boxes, :] = hit.astype(jnp.bfloat16)
    for r, (far, near) in enumerate(sums_of(rows, far_within, slot_within, pick_ref, taken)):
        sums_ref[0, r], sums_ref[1, r] = far, near


def earlier_kernel(prev_ref, far_before, slot_before, pick_ref, sums_ref, out_ref, wide, rows, taken):
    rays, boxes, _ = rows.shape
    rows_of_rays(prev_ref, wide, rows)
    for r, (far, near) in enumerate(sums_of(rows, far_before, slot_before, pick_ref, taken)):
        far = (sums_ref[0, r] + far).astype(jnp.bfloat16).astype(jnp.float32)
        near = (sums_ref[1, r] + near).astype(jnp.bfloat16).astype(jnp.float32)
        wide[pl.ds(r, boxes, stride=rays), :] = far + near
    run = wide.shape[0] // len(CHIPS)
    for n in range(0, len(CHIPS), 2):
        two = [wide[chip * run : (chip + 1) * run, :] for chip in CHIPS[n : n + 2]]
        out_ref[n * run : (n + 2) * run, :] = jnp.concatenate(two, axis=0).astype(jnp.bfloat16)


def body(signal, source_boxes, near_boxes, trans_kernel, near_kernel):
    box_dev, all_rays, width = signal.shape
    devs = lax.axis_size("space")
    rays = all_rays // devs
    boxes = box_dev * devs
    offsets, slots = trans_kernel.shape[0], near_kernel.shape[0]
    mid = box_dev * rays

    split = (box_dev, devs, rays, width)
    parted = pl.pallas_call(
        parts_kernel,
        out_shape=jax.ShapeDtypeStruct((devs, box_dev, rays, width), signal.dtype),
        in_specs=[HBM],
        out_specs=VMEM,
        scratch_shapes=[pltpu.VMEM(split, signal.dtype), pltpu.SemaphoreType.DMA],
        compiler_params=pltpu.CompilerParams(vmem_limit_bytes=4 << 20),
        name="parts",
    )(in_hbm(signal.reshape(split)))
    current = exchange(parted.reshape(devs, mid, width))
    size = lax.axis_size("tm")
    earlier = lax.ppermute(current, "tm", [(i, i + 1) for i in range(size - 1)])

    far_before = jax.ShapeDtypeStruct((rays, offsets * width, width), jnp.bfloat16)
    slot_before = jax.ShapeDtypeStruct((slots * width, width), jnp.bfloat16)
    work = [
        pltpu.VMEM((devs * mid, width), jnp.float32),
        pltpu.VMEM((rays, boxes, width), jnp.bfloat16),
        pltpu.VMEM((rays, boxes, (offsets + slots) * width), jnp.bfloat16),
    ]
    begun = pl.pallas_call(
        current_kernel,
        out_shape=(
            far_before,
            slot_before,
            jax.ShapeDtypeStruct(((offsets + slots) * boxes, boxes), jnp.bfloat16),
            jax.ShapeDtypeStruct((2, rays, boxes, width), jnp.float32),
        ),
        in_specs=[HBM] * 4 + [VMEM],
        out_specs=(VMEM,) * 4,
        scratch_shapes=[
            pltpu.VMEM((offsets, boxes), jnp.int32),
            pltpu.VMEM((slots, boxes), jnp.int32),
            pltpu.VMEM(trans_kernel.shape, jnp.float32),
            pltpu.VMEM(near_kernel.shape, jnp.float32),
            pltpu.SemaphoreType.DMA((4,)),
            pltpu.VMEM(far_before.shape, jnp.bfloat16),
            pltpu.VMEM(slot_before.shape, jnp.bfloat16),
            *work,
        ],
        compiler_params=pltpu.CompilerParams(vmem_limit_bytes=24 << 20),
        cost_estimate=pl.CostEstimate(flops=1_000_000_000, bytes_accessed=6_000_000, transcendentals=0),
        name="current",
    )(
        in_hbm(source_boxes.T),
        in_hbm(near_boxes.T),
        in_hbm(trans_kernel),
        in_hbm(near_kernel),
        current.reshape(devs * mid, width),
    )
    field = pl.pallas_call(
        earlier_kernel,
        out_shape=jax.ShapeDtypeStruct((devs * mid, width), jnp.bfloat16),
        in_specs=[VMEM] * 5,
        out_specs=VMEM,
        scratch_shapes=work,
        compiler_params=pltpu.CompilerParams(vmem_limit_bytes=24 << 20),
        cost_estimate=pl.CostEstimate(flops=1_000_000_000, bytes_accessed=6_000_000, transcendentals=0),
        name="earlier",
    )(earlier.reshape(devs * mid, width), *begun)
    back = exchange(field.reshape(devs, mid, width))
    whole = pl.pallas_call(
        whole_kernel,
        out_shape=jax.ShapeDtypeStruct(split, signal.dtype),
        in_specs=[VMEM],
        out_specs=pl.BlockSpec(memory_space=pl.ANY),
        scratch_shapes=[pltpu.VMEM(split, signal.dtype), pltpu.SemaphoreType.DMA],
        compiler_params=pltpu.CompilerParams(vmem_limit_bytes=4 << 20),
        name="whole",
    )(back.reshape(devs, box_dev, rays, width))
    return whole.reshape(signal.shape)


def solution(mesh):
    in_specs = (P("space", None, "tm"), P(), P(), P(None, "space", None), P())
    out_specs = P("space", None, "tm")
    return jax.shard_map(body, mesh=mesh, in_specs=in_specs, out_specs=out_specs, check_vma=False)
```

```python
import functools

import jax
import jax.numpy as jnp
from jax import lax
from jax.experimental import pallas as pl
from jax.experimental.pallas import tpu as pltpu
from jax.sharding import PartitionSpec as P

VMEM = pl.BlockSpec(memory_space=pltpu.VMEM)
HBM = pl.BlockSpec(memory_space=pltpu.HBM)
Z, Y, CORES = 8, 8, 2
TURNS = (4, 0, 6, 2, 5, 1, 7, 3)
CHIPS = [z * Y + y for y in TURNS for z in TURNS]
RANKS = [chip * CORES + c for chip in CHIPS for c in range(CORES)]


def in_hbm(array):
    return pltpu.with_memory_space_constraint(array, pltpu.HBM)


def exchange(chunks):
    return lax.all_to_all(chunks, "space", split_axis=0, concat_axis=0, axis_index_groups=[RANKS], tiled=True)


def pieces(array_ref):
    boxes, devs = array_ref.shape[:2]
    run = devs // 4
    return [(box, range(first, first + run)) for box in range(boxes) for first in range(0, devs, run)]


def parts_kernel(signal_hbm, parts_ref, signal_ref, sems):
    copies = []
    for n, (box, own) in enumerate(pieces(signal_ref)):
        place = (box, pl.ds(own.start, len(own)))
        copies.append(pltpu.make_async_copy(signal_hbm.at[place], signal_ref.at[place], sems.at[n]))
        copies[-1].start()
    for copy, (box, own) in zip(copies, pieces(signal_ref)):
        copy.wait()
        for dev in own:
            parts_ref[RANKS.index(dev), box] = signal_ref[box, dev]


def whole_kernel(parts_ref, field_hbm, field_ref, sem):
    for rank, dev in enumerate(RANKS):
        for box in range(field_ref.shape[0]):
            field_ref[box, dev] = parts_ref[rank, box]
    copy = pltpu.make_async_copy(field_ref, field_hbm, sem)
    copy.start()
    copy.wait()


def circulant_halves(lags):
    width = lags.shape[-1]
    lags = lags.astype(jnp.bfloat16).astype(jnp.float32)
    turned = pltpu.roll(jnp.broadcast_to(lags, (width, width)), 0, 1, stride=1, stride_axis=0)
    s = lax.broadcasted_iota(jnp.int32, (width, width), 0)
    t = lax.broadcasted_iota(jnp.int32, (width, width), 1)
    before = jnp.where(t < s, turned, 0.0).astype(jnp.bfloat16)
    within = jnp.where(t >= s, turned, 0.0).astype(jnp.bfloat16)
    return before, within


def rows_of_rays(block_ref, wide, rows):
    rays, boxes, _ = rows.shape
    run = wide.shape[0] // len(CHIPS)
    for n in range(0, len(CHIPS), 2):
        two = block_ref[n * run : (n + 2) * run, :].astype(jnp.float32)
        for chip, one in ((CHIPS[n], two[:run]), (CHIPS[n + 1], two[run:])):
            wide[chip * run : (chip + 1) * run, :] = one
    for r in range(rays):
        rows[r] = wide[pl.ds(r, boxes, stride=rays), :].astype(jnp.bfloat16)


def sums_of(rows, far_ref, slot_ref, pick_ref, taken):
    rays, boxes, width = rows.shape
    offsets, slots = far_ref.shape[1] // width, slot_ref.shape[0] // width
    beside = jnp.concatenate([rows[r] for r in range(rays)], axis=1)
    for k in range(offsets + slots):
        got = jnp.dot(pick_ref[k * boxes : (k + 1) * boxes, :], beside, preferred_element_type=jnp.float32)
        got = got.astype(jnp.bfloat16)
        for r in range(rays):
            taken[r, :, k * width : (k + 1) * width] = got[:, r * width : (r + 1) * width]
    cut = offsets * width
    return [
        (
            jnp.dot(taken[r, :, :cut], far_ref[r], preferred_element_type=jnp.float32),
            jnp.dot(taken[r, :, cut:], slot_ref[...], preferred_element_type=jnp.float32),
        )
        for r in range(rays)
    ]


def current_kernel(
    source_hbm, near_hbm, trans_hbm, slot_hbm, cur_ref, far_before, slot_before, pick_ref, sums_ref,
    source_ref, near_ref, trans_ref, slot_ref, sems, far_within, slot_within, wide, rows, taken,
):
    given, held = (source_hbm, near_hbm, trans_hbm, slot_hbm), (source_ref, near_ref, trans_ref, slot_ref)
    copies = [pltpu.make_async_copy(ref, here, sems.at[n]) for n, (ref, here) in enumerate(zip(given, held))]
    for copy in copies:
        copy.start()
    rows_of_rays(cur_ref, wide, rows)
    for copy in copies:
        copy.wait()
    offsets, rays, width = trans_ref.shape
    slots = slot_ref.shape[0]
    boxes = source_ref.shape[1]
    for k in range(offsets):
        for r in range(rays):
            before, within = circulant_halves(trans_ref[k, r : r + 1, :])
            far_before[r, k * width : (k + 1) * width, :] = before
            far_within[r, k * width : (k + 1) * width, :] = within
    for j in range(slots):
        before, within = circulant_halves(slot_ref[j : j + 1, :])
        slot_before[j * width : (j + 1) * width, :] = before
        slot_within[j * width : (j + 1) * width, :] = within
    lane = lax.broadcasted_iota(jnp.int32, (boxes, boxes), 1)
    source = jnp.transpose(source_ref[...])
    near = jnp.transpose(near_ref[...])
    for k in range(offsets + slots):
        column = source[:, k : k + 1] if k < offsets else near[:, k - offsets : k - offsets + 1]
        hit = jnp.where(column == lane, 1.0, 0.0)
        pick_ref[k * boxes : (k + 1) * boxes, :] = hit.astype(jnp.bfloat16)
    for r, (far, near) in enumerate(sums_of(rows, far_within, slot_within, pick_ref, taken)):
        sums_ref[0, r], sums_ref[1, r] = far, near


def earlier_kernel(prev_ref, far_before, slot_before, pick_ref, sums_ref, out_ref, wide, rows, taken):
    rays, boxes, _ = rows.shape
    rows_of_rays(prev_ref, wide, rows)
    for r, (far, near) in enumerate(sums_of(rows, far_before, slot_before, pick_ref, taken)):
        far = (sums_ref[0, r] + far).astype(jnp.bfloat16).astype(jnp.float32)
        near = (sums_ref[1, r] + near).astype(jnp.bfloat16).astype(jnp.float32)
        wide[pl.ds(r, boxes, stride=rays), :] = far + near
    run = wide.shape[0] // len(CHIPS)
    for n in range(0, len(CHIPS), 2):
        two = [wide[chip * run : (chip + 1) * run, :] for chip in CHIPS[n : n + 2]]
        out_ref[n * run : (n + 2) * run, :] = jnp.concatenate(two, axis=0).astype(jnp.bfloat16)


def body(signal, source_boxes, near_boxes, trans_kernel, near_kernel):
    box_dev, all_rays, width = signal.shape
    devs = lax.axis_size("space")
    rays = all_rays // devs
    boxes = box_dev * devs
    offsets, slots = trans_kernel.shape[0], near_kernel.shape[0]
    mid = box_dev * rays

    split = (box_dev, devs, rays, width)
    parted = pl.pallas_call(
        parts_kernel,
        out_shape=jax.ShapeDtypeStruct((devs, box_dev, rays, width), signal.dtype),
        in_specs=[HBM],
        out_specs=VMEM,
        scratch_shapes=[pltpu.VMEM(split, signal.dtype), pltpu.SemaphoreType.DMA((4 * box_dev,))],
        compiler_params=pltpu.CompilerParams(vmem_limit_bytes=4 << 20),
        name="parts",
    )(in_hbm(signal.reshape(split)))
    current = exchange(parted.reshape(devs, mid, width))
    size = lax.axis_size("tm")
    earlier = lax.ppermute(current, "tm", [(i, i + 1) for i in range(size - 1)])

    far_before = jax.ShapeDtypeStruct((rays, offsets * width, width), jnp.bfloat16)
    slot_before = jax.ShapeDtypeStruct((slots * width, width), jnp.bfloat16)
    work = [
        pltpu.VMEM((devs * mid, width), jnp.float32),
        pltpu.VMEM((rays, boxes, width), jnp.bfloat16),
        pltpu.VMEM((rays, boxes, (offsets + slots) * width), jnp.bfloat16),
    ]
    begun = pl.pallas_call(
        current_kernel,
        out_shape=(
            far_before,
            slot_before,
            jax.ShapeDtypeStruct(((offsets + slots) * boxes, boxes), jnp.bfloat16),
            jax.ShapeDtypeStruct((2, rays, boxes, width), jnp.float32),
        ),
        in_specs=[HBM] * 4 + [VMEM],
        out_specs=(VMEM,) * 4,
        scratch_shapes=[
            pltpu.VMEM((offsets, boxes), jnp.int32),
            pltpu.VMEM((slots, boxes), jnp.int32),
            pltpu.VMEM(trans_kernel.shape, jnp.float32),
            pltpu.VMEM(near_kernel.shape, jnp.float32),
            pltpu.SemaphoreType.DMA((4,)),
            pltpu.VMEM(far_before.shape, jnp.bfloat16),
            pltpu.VMEM(slot_before.shape, jnp.bfloat16),
            *work,
        ],
        compiler_params=pltpu.CompilerParams(vmem_limit_bytes=24 << 20),
        cost_estimate=pl.CostEstimate(flops=1_000_000_000, bytes_accessed=6_000_000, transcendentals=0),
        name="current",
    )(
        in_hbm(source_boxes.T),
        in_hbm(near_boxes.T),
        in_hbm(trans_kernel),
        in_hbm(near_kernel),
        current.reshape(devs * mid, width),
    )
    field = pl.pallas_call(
        earlier_kernel,
        out_shape=jax.ShapeDtypeStruct((devs * mid, width), jnp.bfloat16),
        in_specs=[VMEM] * 5,
        out_specs=VMEM,
        scratch_shapes=work,
        compiler_params=pltpu.CompilerParams(vmem_limit_bytes=24 << 20),
        cost_estimate=pl.CostEstimate(flops=1_000_000_000, bytes_accessed=6_000_000, transcendentals=0),
        name="earlier",
    )(earlier.reshape(devs * mid, width), *begun)
    back = exchange(field.reshape(devs, mid, width))
    whole = pl.pallas_call(
        whole_kernel,
        out_shape=jax.ShapeDtypeStruct(split, signal.dtype),
        in_specs=[VMEM],
        out_specs=pl.BlockSpec(memory_space=pl.ANY),
        scratch_shapes=[pltpu.VMEM(split, signal.dtype), pltpu.SemaphoreType.DMA],
        compiler_params=pltpu.CompilerParams(vmem_limit_bytes=4 << 20),
        name="whole",
    )(back.reshape(devs, box_dev, rays, width))
    return whole.reshape(signal.shape)


def solution(mesh):
    in_specs = (P("space", None, "tm"), P(), P(), P(None, "space", None), P())
    out_specs = P("space", None, "tm")
    return jax.shard_map(body, mesh=mesh, in_specs=in_specs, out_specs=out_specs, check_vma=False)
```
